32 devices in a mesh: corpus: 4 (over y, x), blk: 8 (over z, core).
Axes of the slice: x: 2, y: 2, z: 4, core: 2. Of those that a mesh axis runs over, the one named last changes fastest.
Arguments:
- embedding: bfloat16 [8192, 1024], P(('corpus', 'blk'))
- cluster: int32 [8192], P(('corpus', 'blk')), may hold values from 0 to 7, as said below
- order: int32 [8192], P(('corpus', 'blk')), may hold values from 0 to 8191, each once
Outputs:
- nearest: float32 [8192], P(('corpus', 'blk'))
The draws below stay inside these ranges and needn't reach their ends.
Inputs may be any that keep to these rules, and one draw needn't show every extreme that they name: On every device, at most 128 documents have clusters with any one value of cluster mod 4. All devices with the same blk index have one common value that exactly 128 of their documents take. `order`: each number appears once.
All inputs are finite; a program needn't handle non-finite values.
Results may differ from the reference program's by a relative error of at most 0.0013.
Values may be sent and summed in bfloat16 or wider, within the bound.
A program may use at most 128 MiB of HBM per device.

```python
import jax
import jax.numpy as jnp
from jax import lax

E = 1024
DOC_DEV = 256
CLUS_OWN = 2
DOCS = 8192
N_CORPUS = 4
N_BLK = 8


def cluster_table(key):
    devices = N_CORPUS * N_BLK
    base = jax.random.fold_in(key, 4242)
    heavy = jax.random.randint(jax.random.fold_in(base, 1), (N_BLK,), 0, N_CORPUS)
    scores = jax.random.randint(jax.random.fold_in(base, 2), (devices, DOC_DEV), 0, 1 << 16)
    scores = scores * DOC_DEV + jnp.arange(DOC_DEV, dtype=jnp.int32)[None, :]
    ranks = jnp.argsort(jnp.argsort(scores, axis=1), axis=1)
    heavy_dev = jnp.tile(heavy, N_CORPUS)[:, None]
    offset = jax.random.randint(jax.random.fold_in(base, 3), (devices, DOC_DEV), 1, N_CORPUS)
    device_offset = jax.random.randint(jax.random.fold_in(base, 6), (devices, 1), 1, N_CORPUS)
    whole_flag = jax.random.randint(jax.random.fold_in(base, 7), (devices, 1), 0, 2) == 1
    forced = jax.random.randint(jax.random.fold_in(base, 8), (), 0, devices)
    whole_flag = whole_flag | (jnp.arange(devices, dtype=jnp.int32)[:, None] == forced)
    offset = jnp.where(whole_flag, device_offset, offset)
    target = jnp.where(ranks < DOC_DEV // 2, heavy_dev, (heavy_dev + offset) % N_CORPUS)
    first = jax.random.randint(jax.random.fold_in(base, 4), (devices, DOC_DEV), 0, CLUS_OWN)
    second = jax.random.randint(jax.random.fold_in(base, 5), (devices, DOC_DEV), 0, CLUS_OWN)
    return (jnp.minimum(first, second) * N_CORPUS + target).reshape(-1).astype(jnp.int32)


def draw_cluster(key, part):
    return cluster_table(key)


def draw_embedding(key, part):
    labels = cluster_table(key)
    base = jax.random.normal(jax.random.fold_in(key, 91), (DOCS, E), jnp.float32)
    noise = jax.random.normal(jax.random.fold_in(key, 92), (DOCS, E), jnp.float32)
    flags = jax.random.randint(jax.random.fold_in(key, 93), (DOCS,), 0, 2)
    sorted_idx = jnp.argsort(labels, stable=True)
    keys_sorted = labels[sorted_idx]
    prev_idx = jnp.concatenate([sorted_idx[:1], sorted_idx[:-1]])
    same = jnp.concatenate([jnp.zeros((1,), dtype=bool), keys_sorted[1:] == keys_sorted[:-1]])
    copied = same & (flags[sorted_idx] == 1)
    mixed = jnp.where(copied[:, None], 0.6 * base[prev_idx] + 0.8 * noise[sorted_idx], base[sorted_idx])
    positions = jnp.arange(DOCS, dtype=jnp.int32)
    back_step = jax.random.randint(jax.random.fold_in(key, 95), (DOCS,), DOC_DEV, 4 * DOC_DEV)
    source = positions - back_step
    source_safe = jnp.maximum(source, 0)
    far_same = (source >= 0) & (keys_sorted[source_safe] == keys_sorted)
    dup_pick = jax.random.randint(jax.random.fold_in(key, 96), (DOCS,), 0, 5) == 0
    take = far_same & dup_pick
    extra = jax.random.normal(jax.random.fold_in(key, 97), (DOCS, E), jnp.float32)
    mixed = jnp.where(take[:, None], 0.98 * mixed[source_safe] + 0.2 * extra, mixed)
    result = jnp.zeros_like(base).at[sorted_idx].set(mixed)
    return result.astype(jnp.bfloat16)


def setup_inputs(seed: int = 0) -> dict:
    arg_keys = jax.random.split(jax.random.key(seed), 4)
    return {
        "embedding": draw_embedding(jax.random.fold_in(arg_keys[3], 71), 0),
        "cluster": draw_cluster(jax.random.fold_in(arg_keys[3], 71), 0),
        "order": jax.random.permutation(arg_keys[2], DOCS).astype(jnp.int32),
    }


def reference(embedding, cluster, order):
    wide = embedding.astype(jnp.float32)
    unit = (wide * lax.rsqrt(lax.optimization_barrier(jnp.sum(wide * wide, axis=1, keepdims=True)) + 1e-06)).astype(jnp.bfloat16)
    total = unit.shape[0]
    block = min(512, total)

    def one_block(start):
        rows = lax.dynamic_slice_in_dim(unit, start, block, 0)
        keys = lax.dynamic_slice_in_dim(cluster, start, block, 0)
        ranks = lax.dynamic_slice_in_dim(order, start, block, 0)
        sims = lax.dot_general(rows, unit, (((1,), (1,)), ((), ())), preferred_element_type=jnp.float32)
        keep = (keys[:, None] == cluster[None, :]) & (order[None, :] < ranks[:, None])
        return lax.optimization_barrier(jnp.max(jnp.where(keep, sims, jnp.float32(-1.0)), axis=1))
    starts = (jnp.arange(total // block, dtype=jnp.int32) * block).astype(jnp.int32)
    return lax.map(one_block, starts).reshape(-1)
```

```python
import functools

import jax
import jax.numpy as jnp
from jax import lax
from jax.experimental import pallas as pl
from jax.experimental.pallas import tpu as pltpu
from jax.sharding import PartitionSpec as P

CORES = 2
CHUNKS = 2


def flip(value, mask, bits):
    out = 0
    for b in range(bits):
        bit = lax.rem(lax.div(value, 1 << b), 2)
        if mask >> b & 1:
            bit = 1 - bit
        out = out + bit * (1 << b)
    return out


def popcount(d):
    return bin(d).count("1")


def kernel(
    groups,
    places,
    emb_ref,
    clus_ref,
    ord_ref,
    out_ref,
    rows,
    cols,
    rmeta,
    cmeta,
    rclus,
    rord,
    rowacc,
    ownacc,
    colres,
    rowres,
    gotrow,
    gotcol,
    rows_send,
    rows_recv,
    sib_send,
    sib_recv,
    cols_send,
    cols_recv,
    rmeta_send,
    rmeta_recv,
    cmeta_send,
    cmeta_recv,
    rres_send,
    rres_recv,
    cres_send,
    cres_recv,
):
    docs = emb_ref.shape[0]
    part = docs // CHUNKS
    bits = groups.bit_length() - 1
    half = places // 2
    even = places % 2 == 0
    c = lax.axis_index("corpus")
    b = lax.axis_index("blk")
    p = lax.div(b, CORES)
    k = lax.rem(b, CORES)

    def plane(d, j):
        return {"corpus": flip(c, d, bits), "blk": p * CORES + (k if j == 0 else 1 - k)}

    def along(s):
        return {"corpus": c, "blk": lax.rem(p + s + places, places) * CORES + k}

    def meets(position, s):
        if even and s == half:
            return position >= places - half
        return None

    def when(cond, f):
        if cond is None:
            f()
        else:
            pl.when(cond)(f)

    def remote(src, dst, send, recv, device):
        return pltpu.make_async_remote_copy(
            src_ref=src,
            dst_ref=dst,
            send_sem=send,
            recv_sem=recv,
            device_id=device,
            device_id_type=pl.DeviceIdType.MESH,
        )

    def piece(ref, i, t):
        return ref.at[i, pl.ds(t * part, part), :]

    plane_peers = [(d, j) for d in range(groups) for j in range(2) if (d, j) != (0, 0)]
    barrier = pltpu.get_barrier_semaphore()
    for d, j in plane_peers:
        pl.semaphore_signal(barrier, inc=1, device_id=plane(d, j), device_id_type=pl.DeviceIdType.MESH)
    for s in range(1, places):
        pl.semaphore_signal(barrier, inc=1, device_id=along(s), device_id_type=pl.DeviceIdType.MESH)

    def normalise(t):
        wide = emb_ref[pl.ds(t * part, part), :].astype(jnp.float32)
        scale = lax.rsqrt(jnp.sum(wide * wide, axis=1, keepdims=True) + 1e-06)
        rows[0, pl.ds(t * part, part), :] = (wide * scale).astype(jnp.bfloat16)

    def col_copy(s, t):
        src = piece(rows, 0, t) if s == 1 else piece(cols, s - 2, t)
        return remote(src, piece(cols, s - 1, t), cols_send.at[s - 1, t], cols_recv.at[s - 1, t], along(1))

    def col_send(s, t):
        when(meets(lax.rem(p + 1, places), s), lambda: col_copy(s, t).start())

    def via(d, t):
        ones = [1 << i for i in range(bits) if d >> i & 1]
        return ones[t % len(ones)]

    def row_copy(d, t):
        hop = via(d, t)
        return remote(
            piece(rows, 2 * (d ^ hop), t),
            piece(rows, 2 * d, t),
            rows_send.at[d, t],
            rows_recv.at[d, t],
            plane(hop, 0),
        )

    def sib_copy(d, t):
        return remote(
            piece(rows, 2 * d, t), piece(rows, 2 * d + 1, t), sib_send.at[d, t], sib_recv.at[d, t], plane(0, 1)
        )

    def order_of(d):
        first = 0 if d & 1 == 0 else 1
        return [(first + t) % CHUNKS for t in range(CHUNKS)]

    normalise(0)
    rmeta[0] = jnp.concatenate(
        [clus_ref[...], ord_ref[...], jnp.zeros((6, docs), jnp.int32)], axis=0
    ).astype(jnp.float32)
    pl.semaphore_wait(barrier, len(plane_peers) + places - 1)

    singles = [1 << i for i in range(bits)]
    metas = []
    for t in range(CHUNKS):
        if t:
            normalise(t)
        if places > 1:
            col_send(1, t)
        for d in singles:
            if t == order_of(d)[0]:
                row_copy(d, t).start()
        if t == 0:
            for s in range(1, half + 1):
                cp = remote(rmeta.at[0], cmeta.at[s - 1], cmeta_send.at[s - 1], cmeta_recv.at[s - 1], along(s))
                when(meets(lax.rem(p + s, places), s), cp.start)
            for d, j in plane_peers:
                i = 2 * d + j
                cp = remote(rmeta.at[0], rmeta.at[i], rmeta_send.at[i], rmeta_recv.at[i], plane(d, j))
                cp.start()
                metas.append(cp)
        sib_copy(0, t).start()
    for i in range(1, CHUNKS):
        for d in singles:
            row_copy(d, order_of(d)[i]).start()

    def spread(i):
        for row, ref in ((0, rclus), (1, rord)):
            line = jnp.broadcast_to(rmeta[i, row : row + 1, :], (128, docs))
            ref[pl.ds(i * docs, docs), :] = line.T

    spread(0)
    rowacc[...] = jnp.full(rowacc.shape, -1.0, jnp.float32)
    colres[...] = jnp.full(colres.shape, -1.0, jnp.float32)
    ownacc[...] = jnp.full(ownacc.shape, -1.0, jnp.float32)

    def similar(left, right):
        return lax.dot_general(left, right, (((1,), (1,)), ((), ())), preferred_element_type=jnp.float32)

    def fold(x):
        return jnp.max(x.reshape(x.shape[0] // 8, 8, x.shape[1]), axis=0)

    def with_self(i):
        sims = similar(rows[i], rows[0])
        for t in range(docs // 128):
            lanes = slice(t * 128, (t + 1) * 128)
            at = pl.ds(i * docs, docs)
            keep = (rclus[at, :] == rmeta[0, 0:1, lanes]) & (rord[at, :] < rmeta[0, 1:2, lanes])
            ownacc[:, lanes] = jnp.maximum(ownacc[:, lanes], fold(jnp.where(keep, sims[:, lanes], -1.0)))

    def cross(s, t, i):
        lanes = slice(t * part, (t + 1) * part)
        sims = similar(rows[i], cols[s - 1, lanes, :])
        at = pl.ds(pl.multiple_of(i * docs, docs), docs)
        same = jnp.where(rclus[at, :] == cmeta[s - 1, 0:1, lanes], sims, -1.0)
        earlier = cmeta[s - 1, 1:2, lanes] < rord[at, :]
        rowacc[at, :] = jnp.maximum(rowacc[at, :], jnp.where(earlier, same, -1.0))
        colres[s - 1, :, lanes] = jnp.maximum(
            colres[s - 1, :, lanes], fold(jnp.where(earlier, -1.0, same))
        )

    def cross_all(s, t, ds):
        slots = [2 * d + j for d in ds for j in range(2)]
        if slots == list(range(slots[0], slots[0] + len(slots))) and len(slots) > 2:

            @pl.loop(0, len(slots) // 2)
            def _(n):
                cross(s, t, slots[0] + 2 * n)
                cross(s, t, slots[0] + 2 * n + 1)
        else:
            for i in slots:
                cross(s, t, i)

    def wait_cols(s, t):
        col_copy(s, t).wait_recv()
        if s < half:
            col_send(s + 1, t)

    sent_cols = []

    def return_cols(s):
        cp = remote(colres.at[s - 1], gotcol.at[s - 1], cres_send.at[s - 1], cres_recv.at[s - 1], along(-s))
        cp.start()

    rounds = max(bits, half)
    for r in range(rounds + 1):
        now = [d for d in range(groups) if popcount(d) == r]
        here = [d for d in range(groups) if popcount(d) <= r]
        before = [d for d in range(groups) if popcount(d) < r]
        for i in range(CHUNKS):
            if r:
                for d in now:
                    t = order_of(d)[i]
                    row_copy(d, t).wait_recv()
                    for e in range(groups):
                        if popcount(e) == r + 1 and e ^ via(e, t) == d:
                            row_copy(e, t).start()
                    sib_copy(d, t).start()
            if 1 <= r < half:
                wait_cols(r, i)
        if r == 0:
            with_self(0)
            for cp in metas:
                cp.wait_recv()
            for i in range(1, 2 * groups):
                spread(i)
        for d in now:
            for t in range(CHUNKS):
                sib_copy(d, t).wait_recv()
            if r:
                with_self(2 * d)
            with_self(2 * d + 1)
        for s in range(1, min(r, half + 1)):
            if now:

                def older(s=s):
                    for t in range(CHUNKS):
                        cross_all(s, t, now)

                when(meets(p, s), older)
        if 1 <= r <= half:

            def newest(s=r):
                remote(
                    rmeta.at[0], cmeta.at[s - 1], cmeta_send.at[s - 1], cmeta_recv.at[s - 1], along(s)
                ).wait_recv()
                for t in range(CHUNKS):
                    if s >= half:
                        wait_cols(s, t)
                    cross_all(s, t, here)

            when(meets(p, r), newest)
        for s in range(1, half + 1):
            if r == max(s, bits):
                when(meets(p, s), functools.partial(return_cols, s))

    finals = []
    for d in range(groups):
        for j in range(2):
            i = 2 * d + j
            rowres[i] = fold(rowacc[pl.ds(i * docs, docs), :].T)
            if i:
                cp = remote(rowres.at[i], gotrow.at[i], rres_send.at[i], rres_recv.at[i], plane(d, j))
                cp.start()
                finals.append(cp)

    ownacc[...] = jnp.maximum(ownacc[...], rowres[0])
    for s in range(1, half + 1):

        def take(s=s):
            remote(
                colres.at[s - 1], gotcol.at[s - 1], cres_send.at[s - 1], cres_recv.at[s - 1], along(-s)
            ).wait_recv()
            ownacc[...] = jnp.maximum(ownacc[...], gotcol[s - 1])

        when(meets(lax.rem(p + s, places), s), take)
    for i, cp in enumerate(finals):
        cp.wait_recv()
        ownacc[...] = jnp.maximum(ownacc[...], gotrow[i + 1])
    out_ref[...] = jnp.max(ownacc[...], axis=0, keepdims=True)

    for cp in metas + finals:
        cp.wait_send()
    for t in range(CHUNKS):
        for d in range(groups):
            if d:
                row_copy(d, t).wait_send()
            sib_copy(d, t).wait_send()
    for s in range(1, half + 1):

        def sent(s=s):
            for t in range(CHUNKS):
                col_copy(s, t).wait_send()

        def sent_meta(s=s):
            remote(
                rmeta.at[0], cmeta.at[s - 1], cmeta_send.at[s - 1], cmeta_recv.at[s - 1], along(s)
            ).wait_send()

        def sent_back(s=s):
            remote(
                colres.at[s - 1], gotcol.at[s - 1], cres_send.at[s - 1], cres_recv.at[s - 1], along(-s)
            ).wait_send()

        when(meets(lax.rem(p + 1, places), s), sent)
        when(meets(lax.rem(p + s, places), s), sent_meta)
        when(meets(p, s), sent_back)


def local(groups, places, embedding, cluster, order):
    docs, width = embedding.shape
    half = places // 2
    slots = 2 * groups
    dma = pltpu.SemaphoreType.DMA
    out = pl.pallas_call(
        functools.partial(kernel, groups, places),
        out_shape=jax.ShapeDtypeStruct((1, docs), jnp.float32),
        in_specs=[pl.BlockSpec(memory_space=pltpu.VMEM)] * 3,
        out_specs=pl.BlockSpec(memory_space=pltpu.VMEM),
        scratch_shapes=[
            pltpu.VMEM((slots, docs, width), jnp.bfloat16),
            pltpu.VMEM((half, docs, width), jnp.bfloat16),
            pltpu.VMEM((slots, 8, docs), jnp.float32),
            pltpu.VMEM((half, 8, docs), jnp.float32),
            pltpu.VMEM((slots * docs, 128), jnp.float32),
            pltpu.VMEM((slots * docs, 128), jnp.float32),
            pltpu.VMEM((slots * docs, 128), jnp.float32),
            pltpu.VMEM((8, docs), jnp.float32),
            pltpu.VMEM((half, 8, docs), jnp.float32),
            pltpu.VMEM((slots, 8, docs), jnp.float32),
            pltpu.VMEM((slots, 8, docs), jnp.float32),
            pltpu.VMEM((half, 8, docs), jnp.float32),
            dma((groups, CHUNKS)),
            dma((groups, CHUNKS)),
            dma((groups, CHUNKS)),
            dma((groups, CHUNKS)),
            dma((half, CHUNKS)),
            dma((half, CHUNKS)),
            dma((slots,)),
            dma((slots,)),
            dma((half,)),
            dma((half,)),
            dma((slots,)),
            dma((slots,)),
            dma((half,)),
            dma((half,)),
        ],
        compiler_params=pltpu.CompilerParams(
            collective_id=0, has_side_effects=True, vmem_limit_bytes=40 * 2**20
        ),
    )(embedding, cluster.reshape(1, docs), order.reshape(1, docs))
    return out.reshape(docs)


def solution(mesh):
    body = functools.partial(local, mesh.shape["corpus"], mesh.shape["blk"] // CORES)
    in_specs = (P(("corpus", "blk"), None), P(("corpus", "blk")), P(("corpus", "blk")))
    out_specs = P(("corpus", "blk"))
    return jax.shard_map(body, mesh=mesh, in_specs=in_specs, out_specs=out_specs, check_vma=False)
```
